32 devices in a mesh: shard: 4 (over y, core), rep: 8 (over z, x).
Axes of the slice: x: 2, y: 2, z: 4, core: 2. Of those that a mesh axis runs over, the one named last changes fastest.
Arguments:
- inputs: bfloat16 [16384, 1088], P(('shard', 'rep')), may hold values from -6 to 6
- lengths: int32 [32, 8], P(('shard', 'rep')), may hold values from 0 to 512, as said below
- query_weight: bfloat16 [1088, 1088], P('shard'), may hold values from -0.1875 to 0.1875
- key_weight: bfloat16 [1088, 1088], P('shard'), may hold values from -0.1875 to 0.1875
- value_weight: bfloat16 [1088, 1088], P('shard'), may hold values from -0.1875 to 0.1875
- out_weight: bfloat16 [1088, 1088], P('shard'), may hold values from -0.75 to 0.75
- up_weight: bfloat16 [1088, 4352], P('shard'), may hold values from -0.1875 to 0.1875
- down_weight: bfloat16 [4352, 1088], P('shard'), may hold values from -0.09375 to 0.09375
- query_bias: bfloat16 [1088], P('shard'), may hold values from -1 to 1
- value_bias: bfloat16 [1088], P('shard'), may hold values from -1 to 1
- out_bias: bfloat16 [1088], P('shard'), may hold values from -1 to 1
- up_bias: bfloat16 [4352], P('shard'), may hold values from -1 to 1
- down_bias: bfloat16 [1088], P('shard'), may hold values from -1 to 1
- gain_one: bfloat16 [1088], P('shard'), may hold values from 0.5 to 1.5
- bias_one: bfloat16 [1088], P('shard'), may hold values from -1 to 1
- gain_two: bfloat16 [1088], P('shard'), may hold values from 0.5 to 1.5
- bias_two: bfloat16 [1088], P('shard'), may hold values from -1 to 1
- cotangent: bfloat16 [16384, 1088], P(('shard', 'rep')), may hold values from -6 to 6
Outputs:
- outputs: bfloat16 [16384, 1088], P(('shard', 'rep'))
- grad_inputs: bfloat16 [16384, 1088], P(('shard', 'rep'))
- grad_query: float32 [1088, 1088], P('shard')
- grad_key: float32 [1088, 1088], P('shard')
- grad_value: float32 [1088, 1088], P('shard')
- grad_out: float32 [1088, 1088], P('shard')
- grad_up: float32 [1088, 4352], P('shard')
- grad_down: float32 [4352, 1088], P('shard')
- grad_query_bias: float32 [1088], P('shard')
- grad_value_bias: float32 [1088], P('shard')
- grad_out_bias: float32 [1088], P('shard')
- grad_up_bias: float32 [4352], P('shard')
- grad_down_bias: float32 [1088], P('shard')
- grad_gain_one: float32 [1088], P('shard')
- grad_bias_one: float32 [1088], P('shard')
- grad_gain_two: float32 [1088], P('shard')
- grad_bias_two: float32 [1088], P('shard')
The draws below stay inside these ranges and needn't reach their ends.
Inputs may be any that keep to these rules, and one draw needn't show every extreme that they name: Row j lists the lengths of the sequences packed into block j of 512 rows, in order, zeros for empty slots; a row sums to at most 512; in every draw some row holds one sequence of exactly 512.
All inputs are finite; a program needn't handle non-finite values.
Results may differ from the reference program's by a relative error of at most 0.017.
Values may be sent and summed in bfloat16 or wider, within the bound.
A program may use at most 192 MiB of HBM per device.

```python
import jax
import jax.numpy as jnp
from jax import lax

D = 1088
H = 17
HD = 64
FF = 4352
CAP = 512
SLOTS = 8
TOKENS = 16384
N_SHARD = 4
N_REP = 8


def draw_lengths(key, part):
    key = jax.random.fold_in(key, 11)
    key_total, key_cuts, key_pick = jax.random.split(key, 3)
    blocks = N_SHARD * N_REP
    totals = jax.random.randint(key_total, (blocks, 1), CAP // 8, CAP + 1)
    cuts = jax.random.randint(key_cuts, (blocks, SLOTS - 1), 0, CAP + 1)
    cuts = jnp.sort(jnp.minimum(cuts, totals), axis=1)
    edges = jnp.concatenate([jnp.zeros((blocks, 1), jnp.int32), cuts, totals], axis=1)
    pieces = edges[:, 1:] - edges[:, :-1]
    chosen = jax.random.randint(key_pick, (), 0, blocks)
    single = jnp.zeros((SLOTS,), jnp.int32).at[0].set(CAP)
    rowids = jnp.arange(blocks, dtype=jnp.int32)
    pieces = jnp.where(rowids[:, None] == chosen, single[None, :], pieces)
    return pieces.astype(jnp.int32)


def block_scale(stream_key, extent, shards, least, largest):
    loudness = 1.0
    for position, shards_of in shards:
        heights = jax.random.uniform(jax.random.fold_in(jax.random.fold_in(stream_key, 6), position), (shards_of,), jnp.float32, least / len(shards), largest / len(shards))
        loudness = loudness * jnp.repeat(jnp.exp(heights), extent[position] // shards_of).reshape((-1,) + (1,) * (len(extent) - 1 - position))
    return loudness


def centred(own_key, extent, deviation, reach, shards=(), kind=jnp.bfloat16):
    loudness = block_scale(own_key, extent, shards, -0.22, 0.18) if shards else 1.0
    entries = jax.random.normal(own_key, extent, jnp.float32) * deviation * loudness
    return jnp.minimum(jnp.maximum(entries, -reach), reach).astype(kind)


def setup_inputs(seed: int = 0) -> dict:
    key_of = jax.random.split(jax.random.key(seed), 19)
    return {
        "inputs": centred(key_of[0], (TOKENS, D), 1.0, 6.0, ((0, 32),)),
        "lengths": draw_lengths(jax.random.fold_in(key_of[18], 71), 0),
        "query_weight": centred(key_of[2], (D, D), D ** -0.5, 0.1875, ((0, 4),)),
        "key_weight": centred(key_of[3], (D, D), D ** -0.5, 0.1875, ((0, 4),)),
        "value_weight": centred(key_of[4], (D, D), D ** -0.5, 0.1875, ((0, 4),)),
        "out_weight": centred(key_of[5], (D, D), (D // 16) ** -0.5, 0.75, ((0, 4),)),
        "up_weight": centred(key_of[6], (D, FF), D ** -0.5, 0.1875, ((0, 4),)),
        "down_weight": centred(key_of[7], (FF, D), FF ** -0.5, 0.09375, ((0, 4),)),
        "query_bias": centred(key_of[8], (D,), 0.2, 1.0, ((0, 4),)),
        "value_bias": centred(key_of[9], (D,), 0.2, 1.0, ((0, 4),)),
        "out_bias": centred(key_of[10], (D,), 0.2, 1.0, ((0, 4),)),
        "up_bias": centred(key_of[11], (FF,), 0.2, 1.0, ((0, 4),)),
        "down_bias": centred(key_of[12], (D,), 0.2, 1.0, ((0, 4),)),
        "gain_one": jnp.clip(1.0 + 0.1 * jax.random.normal(key_of[13], (D,), jnp.float32), 0.5, 1.5).astype(jnp.bfloat16),
        "bias_one": centred(key_of[14], (D,), 0.2, 1.0, ((0, 4),)),
        "gain_two": jnp.clip(1.0 + 0.1 * jax.random.normal(key_of[15], (D,), jnp.float32), 0.5, 1.5).astype(jnp.bfloat16),
        "bias_two": centred(key_of[16], (D,), 0.2, 1.0, ((0, 4),)),
        "cotangent": centred(key_of[17], (TOKENS, D), 1.0, 6.0, ((0, 32),)),
    }


@jax.custom_vjp
def low(v):
    return lax.optimization_barrier(v.astype(jnp.bfloat16)).astype(jnp.float32)

@jax.custom_vjp
def low_back(v):
    return v

def low_keep(v):
    return (low(v), None)

def low_pass(kept, grad):
    return (grad,)

def back_keep(v):
    return (v, None)

def back_low(kept, grad):
    return (low(grad),)
low.defvjp(low_keep, low_pass)
low_back.defvjp(back_keep, back_low)
epsilon = 1e-05

def normalize(values, gain, shift):
    center = values - lax.optimization_barrier(jnp.mean(values, axis=-1, keepdims=True))
    spread = lax.optimization_barrier(jnp.mean(center * center, axis=-1, keepdims=True))
    return center * lax.rsqrt(spread + epsilon) * gain + shift

def arrange(lengths):
    ends = jnp.cumsum(lengths).astype(jnp.int32)
    rowids = jnp.arange(CAP, dtype=jnp.int32)
    segment = lax.optimization_barrier(jnp.sum((rowids[:, None] >= ends[None, :]).astype(jnp.int32), axis=1)).astype(jnp.int32)
    inside = rowids < ends[-1]
    segment = jnp.where(inside, segment, SLOTS + rowids).astype(jnp.int32)
    return (segment, inside.astype(jnp.float32))

def matmul(left, right):
    return jnp.dot(left, right, preferred_element_type=jnp.float32, precision=lax.Precision.HIGHEST)

def attend(queries, keys, values, segment):
    width = min(512, CAP)
    count = CAP // width
    query_heads = queries.reshape(CAP, H, HD)
    key_heads = keys.reshape(CAP, H, HD)
    value_heads = values.reshape(CAP, H, HD)
    key_rows = jnp.arange(CAP, dtype=jnp.int32)

    def block(index):
        start = (index * width).astype(jnp.int32)
        query_block = lax.dynamic_slice_in_dim(query_heads, start, width, 0)
        query_segment = lax.dynamic_slice_in_dim(segment, start, width, 0)
        query_rows = start + jnp.arange(width, dtype=jnp.int32)
        allowed = (query_segment[:, None] == segment[None, :]) & (query_rows[:, None] >= key_rows[None, :])
        scores = low_back(jnp.einsum('qhd,khd->hqk', query_block, key_heads, precision=lax.Precision.HIGHEST)) * 0.125
        scores = jnp.where(allowed[None], scores, -1e+30)
        highest = lax.optimization_barrier(jnp.max(scores, axis=-1, keepdims=True))
        expo = jnp.exp(scores - highest)
        probs = expo / lax.optimization_barrier(jnp.sum(expo, axis=-1, keepdims=True))
        return jnp.einsum('hqk,khd->qhd', low(probs), value_heads, precision=lax.Precision.HIGHEST)
    blocks = lax.map(jax.checkpoint(block), jnp.arange(count, dtype=jnp.int32))
    return blocks.reshape(CAP, D)

def layer(residual, params, segment, inside):
    query_weight, key_weight, value_weight, out_weight, up_weight, down_weight, query_bias, value_bias, out_bias, up_bias, down_bias, gain_one, bias_one, gain_two, bias_two = params
    normed_one = low(normalize(residual, gain_one, bias_one))
    queries = low(low_back(matmul(normed_one, query_weight) + query_bias))
    keys = low(low_back(matmul(normed_one, key_weight)))
    values = low(low_back(matmul(normed_one, value_weight) + value_bias))
    mixed = low(low_back(attend(queries, keys, values, segment)))
    middle = residual + low_back(matmul(mixed, out_weight) + out_bias)
    normed_two = low(normalize(middle, gain_two, bias_two))
    pre = low_back(matmul(normed_two, up_weight) + up_bias)
    hidden = low(jax.nn.gelu(pre, approximate=False))
    result = middle + low_back(matmul(hidden, down_weight) + down_bias)
    return result * inside[:, None]

def reference(inputs, lengths, query_weight, key_weight, value_weight, out_weight, up_weight, down_weight, query_bias, value_bias, out_bias, up_bias, down_bias, gain_one, bias_one, gain_two, bias_two, cotangent):
    params = tuple((item.astype(jnp.float32) for item in (query_weight, key_weight, value_weight, out_weight, up_weight, down_weight, query_bias, value_bias, out_bias, up_bias, down_bias, gain_one, bias_one, gain_two, bias_two)))
    blocks_in = inputs.astype(jnp.float32).reshape(N_SHARD * N_REP, CAP, D)
    blocks_cot = cotangent.astype(jnp.float32).reshape(N_SHARD * N_REP, CAP, D)

    def step(carry, item):
        residual, upstream, block_lengths = item
        segment, inside = arrange(block_lengths)
        result, pull = jax.vjp(lambda rows, weights: layer(rows, weights, segment, inside), residual, params)
        grad_rows, grad_params = pull(upstream)
        carry = tuple((total + low(term) for total, term in zip(carry, grad_params)))
        return (carry, (result.astype(jnp.bfloat16), grad_rows.astype(jnp.bfloat16)))
    start = tuple((jnp.zeros_like(item) for item in params))
    grads, (results, grad_rows) = lax.scan(step, start, (blocks_in, blocks_cot, lengths))
    return (results.reshape(TOKENS, D), grad_rows.reshape(TOKENS, D), grads[0], grads[1], grads[2], grads[3], grads[4], grads[5], grads[6], grads[7], grads[8], grads[9], grads[10], grads[11], grads[12], grads[13], grads[14])
```

```python
from functools import partial

import jax
import jax.numpy as jnp
from jax import lax
from jax.sharding import PartitionSpec as P

H = 17
HD = 64


epsilon = 1e-05


def normalize(values, gain, shift):
    center = values - jnp.mean(values, axis=-1, keepdims=True)
    spread = jnp.mean(center * center, axis=-1, keepdims=True)
    return center * lax.rsqrt(spread + epsilon) * gain + shift


def arrange(lengths, count):
    ends = jnp.cumsum(lengths)
    rowids = jnp.arange(count, dtype=jnp.int32)
    segment = jnp.sum((rowids[:, None] >= ends[None, :]).astype(jnp.int32), axis=1)
    inside = rowids < ends[-1]
    segment = jnp.where(inside, segment, lengths.shape[0] + rowids)
    return (segment, inside.astype(jnp.float32))


def outer(left, right):
    return lax.dot_general(
        left, right, (((0,), (0,)), ((), ())), preferred_element_type=jnp.float32
    )


def inner(left, right):
    return lax.dot_general(
        left, right, (((1,), (1,)), ((), ())), preferred_element_type=jnp.float32
    )


def block_scores(query_block, key_heads, query_segment, segment, start, width):
    key_rows = jnp.arange(segment.shape[0], dtype=jnp.int32)
    query_rows = start + jnp.arange(width, dtype=jnp.int32)
    allowed = (query_segment[:, None] == segment[None, :]) & (
        query_rows[:, None] >= key_rows[None, :]
    )
    scores = (
        jnp.einsum("qhd,khd->hqk", query_block, key_heads, preferred_element_type=jnp.float32)
        * 0.125
    )
    return jnp.where(allowed[None], scores, -1e30)


def attend_forward(queries, keys, values, segment):
    count = queries.shape[0]
    width = min(512, count)
    query_heads = queries.reshape(count, H, HD)
    key_heads = keys.reshape(count, H, HD)
    value_heads = values.reshape(count, H, HD)

    def block(index):
        start = index * width
        scores = block_scores(query_heads, key_heads, segment, segment, start, width)
        highest = jnp.max(scores, axis=-1, keepdims=True)
        expo = jnp.exp(scores - highest)
        total = jnp.sum(expo, axis=-1, keepdims=True)
        weights = (expo / total).astype(jnp.bfloat16)
        result = jnp.einsum(
            "hqk,khd->qhd", weights, value_heads, preferred_element_type=jnp.float32
        )
        return (result, (highest + jnp.log(total))[..., 0])

    results, logsums = lax.map(block, jnp.arange(count // width, dtype=jnp.int32))
    return (results.reshape(count, H * HD), logsums)


def attend_backward(queries, keys, values, segment, logsums, grad_mixed):
    count = queries.shape[0]
    width = min(512, count)
    query_heads = queries.reshape(count, H, HD)
    key_heads = keys.reshape(count, H, HD)
    value_heads = values.reshape(count, H, HD)
    grad_heads = grad_mixed.reshape(count, H, HD)

    def block(carry, index):
        grad_keys, grad_values = carry
        start = index * width
        scores = block_scores(query_heads, key_heads, segment, segment, start, width)
        probs = jnp.exp(scores - logsums[index][:, :, None])
        grad_values = grad_values + jnp.einsum(
            "hqk,qhd->khd",
            probs.astype(jnp.bfloat16),
            grad_heads,
            preferred_element_type=jnp.float32,
        )
        grad_probs = jnp.einsum(
            "qhd,khd->hqk", grad_heads, value_heads, preferred_element_type=jnp.float32
        )
        grad_scores = probs * (grad_probs - jnp.sum(probs * grad_probs, axis=-1, keepdims=True))
        grad_scores = (grad_scores * 0.125).astype(jnp.bfloat16)
        grad_query_block = jnp.einsum(
            "hqk,khd->qhd", grad_scores, key_heads, preferred_element_type=jnp.float32
        )
        grad_keys = grad_keys + jnp.einsum(
            "hqk,qhd->khd", grad_scores, query_heads, preferred_element_type=jnp.float32
        )
        return ((grad_keys, grad_values), grad_query_block)

    start_value = jnp.zeros((count, H, HD), jnp.float32)
    (grad_keys, grad_values), grad_queries = lax.scan(
        block, (start_value, start_value), jnp.arange(count // width, dtype=jnp.int32)
    )
    return (
        grad_queries.reshape(count, H * HD).astype(jnp.bfloat16),
        grad_keys.reshape(count, H * HD).astype(jnp.bfloat16),
        grad_values.reshape(count, H * HD).astype(jnp.bfloat16),
    )


def column_sum(values):
    return jnp.sum(values.astype(jnp.float32), axis=0)


def swap(value, axis, bit):
    size = lax.axis_size(axis)
    return lax.ppermute(value, axis, [(i, i ^ bit) for i in range(size)])


def has_bit(axis, bit):
    return (lax.axis_index(axis) // bit) % 2


def halve(value, axis, bit, dim):
    mine = has_bit(axis, bit)
    half = value.shape[dim] // 2
    keep = lax.dynamic_slice_in_dim(value, mine * half, half, dim)
    give = lax.dynamic_slice_in_dim(value, (1 - mine) * half, half, dim)
    got = swap(give, axis, bit)
    return (keep.astype(jnp.float32) + got.astype(jnp.float32)).astype(value.dtype)


def double(value, axis, bit, dim):
    got = swap(value, axis, bit)
    mine = has_bit(axis, bit)
    first = jnp.where(mine == 0, value, got)
    second = jnp.where(mine == 0, got, value)
    return jnp.concatenate([first, second], axis=dim)


def exchange_sum(value, axis, bit):
    return (value.astype(jnp.float32) + swap(value, axis, bit).astype(jnp.float32)).astype(
        value.dtype
    )


def reduce_owned(term, first_dim, second_dim):
    shards_count = lax.axis_size("shard")
    rep_count = lax.axis_size("rep")
    trailing = term.shape[1:]
    bits = []
    bit = 1
    while bit < shards_count:
        bits.append(bit)
        bit *= 2
    term = term.reshape((2,) * len(bits) + trailing)
    for place, bit in enumerate(bits):
        dim = len(bits) - 1 - place
        term = halve(term, "shard", bit, dim)
    term = term.reshape(trailing)
    split = []
    bit = 1
    while bit < rep_count:
        if len(split) < 2:
            dim = (first_dim, second_dim)[len(split)]
            term = halve(term, "rep", bit, dim)
            split.append((bit, dim))
        else:
            term = exchange_sum(term, "rep", bit)
        bit *= 2
    for bit, dim in reversed(split):
        term = double(term, "rep", bit, dim)
    return term.astype(jnp.float32)


def reduce_small(term):
    for axis in ("shard", "rep"):
        bit = 1
        while bit < lax.axis_size(axis):
            term = exchange_sum(term, axis, bit)
            bit *= 2
    return lax.dynamic_index_in_dim(term, lax.axis_index("shard"), 0, keepdims=False)


def shards(
    inputs,
    lengths,
    query_weight,
    key_weight,
    value_weight,
    out_weight,
    up_weight,
    down_weight,
    query_bias,
    value_bias,
    out_bias,
    up_bias,
    down_bias,
    gain_one,
    bias_one,
    gain_two,
    bias_two,
    cotangent,
):
    segment, inside = arrange(lengths[0], inputs.shape[0])
    attention_parts = (
        lax.all_gather(query_weight, "shard", axis=0, tiled=True),
        lax.all_gather(key_weight, "shard", axis=0, tiled=True),
        lax.all_gather(value_weight, "shard", axis=0, tiled=True),
        lax.all_gather(out_weight, "shard", axis=0, tiled=True),
        lax.all_gather(query_bias, "shard", axis=0, tiled=True),
        lax.all_gather(value_bias, "shard", axis=0, tiled=True),
        lax.all_gather(out_bias, "shard", axis=0, tiled=True),
        lax.all_gather(gain_one, "shard", axis=0, tiled=True),
        lax.all_gather(bias_one, "shard", axis=0, tiled=True),
    )
    full_query, full_key, full_value, full_out = (
        attention_parts[0],
        attention_parts[1],
        attention_parts[2],
        attention_parts[3],
    )
    query_shift = attention_parts[4].astype(jnp.float32)
    value_shift = attention_parts[5].astype(jnp.float32)
    out_shift = attention_parts[6].astype(jnp.float32)
    first_gain = attention_parts[7].astype(jnp.float32)
    first_shift = attention_parts[8].astype(jnp.float32)
    residual = inputs.astype(jnp.float32)
    normed_one = normalize(residual, first_gain, first_shift).astype(jnp.bfloat16)
    queries = (
        jnp.dot(normed_one, full_query, preferred_element_type=jnp.float32) + query_shift
    ).astype(jnp.bfloat16)
    keys = jnp.dot(normed_one, full_key, preferred_element_type=jnp.float32).astype(jnp.bfloat16)
    values = (
        jnp.dot(normed_one, full_value, preferred_element_type=jnp.float32) + value_shift
    ).astype(jnp.bfloat16)
    mixed_float, logsums = attend_forward(queries, keys, values, segment)
    mixed = mixed_float.astype(jnp.bfloat16)
    middle = residual + jnp.dot(mixed, full_out, preferred_element_type=jnp.float32) + out_shift
    network_parts = (
        lax.all_gather(up_weight, "shard", axis=0, tiled=True),
        lax.all_gather(down_weight, "shard", axis=0, tiled=True),
        lax.all_gather(up_bias, "shard", axis=0, tiled=True),
        lax.all_gather(down_bias, "shard", axis=0, tiled=True),
        lax.all_gather(gain_two, "shard", axis=0, tiled=True),
        lax.all_gather(bias_two, "shard", axis=0, tiled=True),
    )
    full_up, full_down = (network_parts[0], network_parts[1])
    up_shift = network_parts[2].astype(jnp.float32)
    down_shift = network_parts[3].astype(jnp.float32)
    second_gain = network_parts[4].astype(jnp.float32)
    second_shift = network_parts[5].astype(jnp.float32)
    normed_two = normalize(middle, second_gain, second_shift).astype(jnp.bfloat16)
    pre_hidden = jnp.dot(normed_two, full_up, preferred_element_type=jnp.float32) + up_shift
    hidden = jax.nn.gelu(pre_hidden, approximate=False).astype(jnp.bfloat16)
    result = middle + jnp.dot(hidden, full_down, preferred_element_type=jnp.float32) + down_shift
    outputs = (result * inside[:, None]).astype(jnp.bfloat16)
    network_back = (
        lax.all_gather(up_weight, "shard", axis=0, tiled=True),
        lax.all_gather(down_weight, "shard", axis=0, tiled=True),
    )
    back_up, back_down = (network_back[0], network_back[1])
    upstream = cotangent.astype(jnp.float32) * inside[:, None]
    upstream_low = upstream.astype(jnp.bfloat16)
    grad_down_term = outer(hidden, upstream_low)
    grad_hidden = inner(upstream_low, back_down)
    _, gelu_pull = jax.vjp(partial(jax.nn.gelu, approximate=False), pre_hidden)
    grad_pre = gelu_pull(grad_hidden)[0].astype(jnp.bfloat16)
    grad_up_term = outer(normed_two, grad_pre)
    grad_normed_two = inner(grad_pre, back_up)
    _, second_pull = jax.vjp(normalize, middle, second_gain, second_shift)
    grad_middle_norm, grad_second_gain, grad_second_shift = second_pull(grad_normed_two)
    grad_middle = upstream + grad_middle_norm
    count = lax.axis_size("shard")
    down_total = reduce_owned(
        grad_down_term.astype(jnp.bfloat16).reshape(count, -1, grad_down_term.shape[1]), 0, 0
    )
    up_total = reduce_owned(
        grad_up_term.astype(jnp.bfloat16).reshape(count, -1, grad_up_term.shape[1]), 0, 1
    )
    attention_back = (
        lax.all_gather(query_weight, "shard", axis=0, tiled=True),
        lax.all_gather(key_weight, "shard", axis=0, tiled=True),
        lax.all_gather(value_weight, "shard", axis=0, tiled=True),
        lax.all_gather(out_weight, "shard", axis=0, tiled=True),
    )
    back_query, back_key, back_value, back_out = (
        attention_back[0],
        attention_back[1],
        attention_back[2],
        attention_back[3],
    )
    grad_branch = grad_middle.astype(jnp.bfloat16)
    grad_out_term = outer(mixed, grad_branch)
    grad_mixed = inner(grad_branch, back_out).astype(jnp.bfloat16)
    grad_queries, grad_keys, grad_values = attend_backward(
        queries, keys, values, segment, logsums, grad_mixed
    )
    grad_query_term = outer(normed_one, grad_queries)
    grad_key_term = outer(normed_one, grad_keys)
    grad_value_term = outer(normed_one, grad_values)
    grad_normed_one = (
        inner(grad_queries, back_query)
        + inner(grad_keys, back_key)
        + inner(grad_values, back_value)
    )
    _, first_pull = jax.vjp(normalize, residual, first_gain, first_shift)
    grad_residual_norm, grad_first_gain, grad_first_shift = first_pull(grad_normed_one)
    grad_inputs = (grad_middle + grad_residual_norm).astype(jnp.bfloat16)

    def paired(one, two):
        width = one.shape[1]
        return jnp.stack(
            [
                one.astype(jnp.bfloat16).reshape(count, -1, width),
                two.astype(jnp.bfloat16).reshape(count, -1, width),
            ],
            axis=1,
        )

    first_pair = reduce_owned(paired(grad_out_term, grad_value_term), 1, 0)
    second_pair = reduce_owned(paired(grad_query_term, grad_key_term), 1, 0)
    small = [
        column_sum(grad_queries),
        column_sum(grad_values),
        column_sum(grad_branch),
        column_sum(grad_pre),
        column_sum(upstream_low),
        grad_first_gain,
        grad_first_shift,
        grad_second_gain,
        grad_second_shift,
    ]
    widths = [item.shape[0] // count for item in small]
    packed = jnp.concatenate(
        [item.astype(jnp.bfloat16).astype(jnp.float32).reshape(count, -1) for item in small],
        axis=1,
    )
    owned = reduce_small(packed)
    pieces = []
    start = 0
    for width in widths:
        pieces.append(owned[start : start + width])
        start += width
    return (
        outputs,
        grad_inputs,
        second_pair[0],
        second_pair[1],
        first_pair[1],
        first_pair[0],
        up_total,
        down_total,
        *pieces,
    )


def solution(mesh):
    return jax.shard_map(
        shards,
        mesh=mesh,
        in_specs=(
            P(("shard", "rep"), None),
            P(("shard", "rep"), None),
            P("shard", None),
            P("shard", None),
            P("shard", None),
            P("shard", None),
            P("shard", None),
            P("shard", None),
            P("shard"),
            P("shard"),
            P("shard"),
            P("shard"),
            P("shard"),
            P("shard"),
            P("shard"),
            P("shard"),
            P("shard"),
            P(("shard", "rep"), None),
        ),
        out_specs=(
            P(("shard", "rep"), None),
            P(("shard", "rep"), None),
            P("shard", None),
            P("shard", None),
            P("shard", None),
            P("shard", None),
            P("shard", None),
            P("shard", None),
            P("shard"),
            P("shard"),
            P("shard"),
            P("shard"),
            P("shard"),
            P("shard"),
            P("shard"),
            P("shard"),
            P("shard"),
        ),
        check_vma=False,
    )
```

```python
from functools import partial

import jax
import jax.numpy as jnp
from jax import lax
from jax.sharding import PartitionSpec as P

H = 17
HD = 64


epsilon = 1e-05


def normalize(values, gain, shift):
    center = values - jnp.mean(values, axis=-1, keepdims=True)
    spread = jnp.mean(center * center, axis=-1, keepdims=True)
    return center * lax.rsqrt(spread + epsilon) * gain + shift


def arrange(lengths, count):
    ends = jnp.cumsum(lengths)
    rowids = jnp.arange(count, dtype=jnp.int32)
    segment = jnp.sum((rowids[:, None] >= ends[None, :]).astype(jnp.int32), axis=1)
    inside = rowids < ends[-1]
    segment = jnp.where(inside, segment, lengths.shape[0] + rowids)
    return (segment, inside.astype(jnp.float32))


def outer(left, right):
    return lax.dot_general(
        left, right, (((0,), (0,)), ((), ())), preferred_element_type=jnp.float32
    )


def inner(left, right):
    return lax.dot_general(
        left, right, (((1,), (1,)), ((), ())), preferred_element_type=jnp.float32
    )


def block_scores(query_block, key_heads, query_segment, segment, start, width):
    key_rows = jnp.arange(segment.shape[0], dtype=jnp.int32)
    query_rows = start + jnp.arange(width, dtype=jnp.int32)
    allowed = (query_segment[:, None] == segment[None, :]) & (
        query_rows[:, None] >= key_rows[None, :]
    )
    scores = (
        jnp.einsum("qhd,khd->hqk", query_block, key_heads, preferred_element_type=jnp.float32)
        * 0.125
    )
    return jnp.where(allowed[None], scores, -1e30)


def attend_forward(queries, keys, values, segment):
    count = queries.shape[0]
    width = min(512, count)
    query_heads = queries.reshape(count, H, HD)
    key_heads = keys.reshape(count, H, HD)
    value_heads = values.reshape(count, H, HD)

    def block(index):
        start = index * width
        scores = block_scores(query_heads, key_heads, segment, segment, start, width)
        highest = jnp.max(scores, axis=-1, keepdims=True)
        expo = jnp.exp(scores - highest)
        total = jnp.sum(expo, axis=-1, keepdims=True)
        weights = (expo / total).astype(jnp.bfloat16)
        result = jnp.einsum(
            "hqk,khd->qhd", weights, value_heads, preferred_element_type=jnp.float32
        )
        return (result, (highest + jnp.log(total))[..., 0])

    results, logsums = lax.map(block, jnp.arange(count // width, dtype=jnp.int32))
    return (results.reshape(count, H * HD), logsums)


def column_sum(values):
    return jnp.sum(values.astype(jnp.float32), axis=0)


def swap(value, axis, bit):
    size = lax.axis_size(axis)
    return lax.ppermute(value, axis, [(i, i ^ bit) for i in range(size)])


def has_bit(axis, bit):
    return (lax.axis_index(axis) // bit) % 2


def tie(*values):
    return lax.optimization_barrier(values)


def halve(value, axis, bit, dim):
    mine = has_bit(axis, bit)
    half = value.shape[dim] // 2
    keep = lax.dynamic_slice_in_dim(value, mine * half, half, dim)
    give = lax.dynamic_slice_in_dim(value, (1 - mine) * half, half, dim)
    got = swap(give, axis, bit)
    return (keep.astype(jnp.float32) + got.astype(jnp.float32)).astype(value.dtype)


def double(value, axis, bit, dim):
    got = swap(value, axis, bit)
    mine = has_bit(axis, bit)
    first = jnp.where(mine == 0, value, got)
    second = jnp.where(mine == 0, got, value)
    return jnp.concatenate([first, second], axis=dim)


def exchange_sum(value, axis, bit):
    return (value.astype(jnp.float32) + swap(value, axis, bit).astype(jnp.float32)).astype(
        value.dtype
    )


def core_stage(term):
    return halve(term.astype(jnp.bfloat16), "shard", 1, 1)


def y_stage(term):
    return halve(term, "shard", 2, 0)


def x_stage(term, dim):
    return halve(term, "rep", 1, dim)


def rest_stage(term, x_dim, z_dim):
    term = halve(term, "rep", 2, z_dim)
    bit = 4
    while bit < lax.axis_size("rep"):
        term = exchange_sum(term, "rep", bit)
        bit *= 2
    term = double(term, "rep", 2, z_dim)
    term = double(term, "rep", 1, x_dim)
    return term.reshape(term.shape[2:]).astype(jnp.float32)


def reduce_small(term):
    for axis in ("shard", "rep"):
        bit = 1
        while bit < lax.axis_size(axis):
            term = exchange_sum(term, axis, bit)
            bit *= 2
    return lax.dynamic_index_in_dim(term, lax.axis_index("shard"), 0, keepdims=False)


def place(blocks):
    me = lax.axis_index("shard")
    rows = blocks[0].shape[0]
    full = jnp.zeros((rows * len(blocks),) + blocks[0].shape[1:], blocks[0].dtype)
    for offset, block in enumerate(blocks):
        full = lax.dynamic_update_slice_in_dim(full, block, (me ^ offset) * rows, 0)
    return full


def fetch_half(own):
    half = own.shape[0] // 2
    give = lax.dynamic_slice_in_dim(own, has_bit("rep", 1) * half, half, 0)
    return swap(give, "shard", 2)


def spread(own, got):
    sibling = swap(own, "shard", 1)
    remote = double(got, "rep", 1, 0)
    remote_sibling = swap(remote, "shard", 1)
    return place([own, sibling, remote, remote_sibling])


def shards(
    inputs,
    lengths,
    query_weight,
    key_weight,
    value_weight,
    out_weight,
    up_weight,
    down_weight,
    query_bias,
    value_bias,
    out_bias,
    up_bias,
    down_bias,
    gain_one,
    bias_one,
    gain_two,
    bias_two,
    cotangent,
):
    segment, inside = arrange(lengths[0], inputs.shape[0])
    count = lax.axis_size("shard")
    vectors = [
        query_bias,
        value_bias,
        out_bias,
        gain_one,
        bias_one,
        up_bias,
        down_bias,
        gain_two,
        bias_two,
    ]
    pack = jnp.concatenate(vectors)[None]
    pack_far = swap(pack, "shard", 2)
    pack_near = swap(jnp.concatenate([pack, pack_far]), "shard", 1)
    pack_all = place([pack, pack_near[:1], pack_far, pack_near[1:]]).astype(jnp.float32)
    shifts = []
    start = 0
    for item in vectors:
        shifts.append(pack_all[:, start : start + item.shape[0]].reshape(-1))
        start += item.shape[0]
    query_shift, value_shift, out_shift, first_gain, first_shift = shifts[:5]
    up_shift, down_shift, second_gain, second_shift = shifts[5:]
    got_query, got_key, got_value = (fetch_half(w) for w in (query_weight, key_weight, value_weight))
    full_query = spread(query_weight, got_query)
    full_key = spread(key_weight, got_key)
    full_value = spread(value_weight, got_value)
    got_query, got_key, got_value, out_later, up_later = tie(
        got_query, got_key, got_value, out_weight, up_weight
    )
    got_out, got_up = fetch_half(out_later), fetch_half(up_later)
    full_out = spread(out_later, got_out)
    full_up = spread(up_later, got_up)
    got_up, down_later = tie(got_up, down_weight)
    full_down = spread(down_later, fetch_half(down_later))
    residual = inputs.astype(jnp.float32)
    normed_one = normalize(residual, first_gain, first_shift).astype(jnp.bfloat16)
    queries = (
        jnp.dot(normed_one, full_query, preferred_element_type=jnp.float32) + query_shift
    ).astype(jnp.bfloat16)
    keys = jnp.dot(normed_one, full_key, preferred_element_type=jnp.float32).astype(jnp.bfloat16)
    values = (
        jnp.dot(normed_one, full_value, preferred_element_type=jnp.float32) + value_shift
    ).astype(jnp.bfloat16)
    mixed_float, logsums = attend_forward(queries, keys, values, segment)
    mixed = mixed_float.astype(jnp.bfloat16)
    middle = residual + jnp.dot(mixed, full_out, preferred_element_type=jnp.float32) + out_shift
    normed_two = normalize(middle, second_gain, second_shift).astype(jnp.bfloat16)
    pre_hidden = jnp.dot(normed_two, full_up, preferred_element_type=jnp.float32) + up_shift
    hidden = jax.nn.gelu(pre_hidden, approximate=False).astype(jnp.bfloat16)
    upstream = cotangent.astype(jnp.float32) * inside[:, None]
    upstream_low = upstream.astype(jnp.bfloat16)

    def split(term):
        return term.astype(jnp.bfloat16).reshape(2, 2, -1, term.shape[1])

    def paired(one, two):
        return jnp.stack([split(one), split(two)], axis=2)

    down_sum = split(outer(hidden, upstream_low))
    down_sum, full_down = tie(down_sum, full_down)
    down_sum = core_stage(down_sum)
    result = middle + jnp.dot(hidden, full_down, preferred_element_type=jnp.float32) + down_shift
    outputs = (result * inside[:, None]).astype(jnp.bfloat16)
    grad_hidden = inner(upstream_low, full_down)
    _, gelu_pull = jax.vjp(partial(jax.nn.gelu, approximate=False), pre_hidden)
    grad_pre = gelu_pull(grad_hidden)[0].astype(jnp.bfloat16)
    down_sum, grad_pre, outputs = tie(down_sum, grad_pre, outputs)
    down_sum = y_stage(down_sum)
    up_sum = split(outer(normed_two, grad_pre))
    up_sum, grad_pre = tie(up_sum, grad_pre)
    up_sum = core_stage(up_sum)
    grad_normed_two = inner(grad_pre, full_up)
    _, second_pull = jax.vjp(normalize, middle, second_gain, second_shift)
    grad_middle_norm, grad_second_gain, grad_second_shift = second_pull(grad_normed_two)
    grad_middle = upstream + grad_middle_norm
    grad_branch = grad_middle.astype(jnp.bfloat16)
    grad_out_term = outer(mixed, grad_branch)
    up_sum, grad_branch = tie(up_sum, grad_branch)
    up_sum = x_stage(up_sum, 2)
    grad_mixed = inner(grad_branch, full_out).astype(jnp.bfloat16)

    width = queries.shape[0]
    query_heads = queries.reshape(width, H, HD)
    key_heads = keys.reshape(width, H, HD)
    value_heads = values.reshape(width, H, HD)
    grad_heads = grad_mixed.reshape(width, H, HD)
    scores = block_scores(query_heads, key_heads, segment, segment, 0, width)
    probs = jnp.exp(scores - logsums[0][:, :, None])
    grad_values = jnp.einsum(
        "hqk,qhd->khd",
        probs.astype(jnp.bfloat16),
        grad_heads,
        preferred_element_type=jnp.float32,
    ).reshape(width, H * HD).astype(jnp.bfloat16)
    pair_one = paired(grad_out_term, outer(normed_one, grad_values))
    pair_one, grad_heads = tie(pair_one, grad_heads)
    pair_one = core_stage(pair_one)
    grad_probs = jnp.einsum(
        "qhd,khd->hqk", grad_heads, value_heads, preferred_element_type=jnp.float32
    )
    grad_scores = probs * (grad_probs - jnp.sum(probs * grad_probs, axis=-1, keepdims=True))
    grad_scores = (grad_scores * 0.125).astype(jnp.bfloat16)
    down_sum, up_sum, pair_one, grad_scores = tie(down_sum, up_sum, pair_one, grad_scores)
    down_sum = x_stage(down_sum, 2)
    up_sum = y_stage(up_sum)
    grad_queries = jnp.einsum(
        "hqk,khd->qhd", grad_scores, key_heads, preferred_element_type=jnp.float32
    ).reshape(width, H * HD).astype(jnp.bfloat16)
    grad_keys = jnp.einsum(
        "hqk,qhd->khd", grad_scores, query_heads, preferred_element_type=jnp.float32
    ).reshape(width, H * HD).astype(jnp.bfloat16)
    pair_two = paired(outer(normed_one, grad_queries), outer(normed_one, grad_keys))
    pair_two, down_sum, grad_queries, grad_keys = tie(
        pair_two, down_sum, grad_queries, grad_keys
    )
    pair_two = core_stage(pair_two)
    grad_normed_one = (
        inner(grad_queries, full_query)
        + inner(grad_keys, full_key)
        + inner(grad_values, full_value)
    )
    _, first_pull = jax.vjp(normalize, residual, first_gain, first_shift)
    grad_residual_norm, grad_first_gain, grad_first_shift = first_pull(grad_normed_one)
    grad_inputs = (grad_middle + grad_residual_norm).astype(jnp.bfloat16)
    down_total = rest_stage(down_sum, 2, 2)
    up_total = rest_stage(up_sum, 2, 3)
    pair_one = rest_stage(x_stage(y_stage(pair_one), 3), 3, 2)
    pair_two = rest_stage(y_stage(x_stage(pair_two, 3)), 3, 2)
    small = [
        column_sum(grad_queries),
        column_sum(grad_values),
        column_sum(grad_branch),
        column_sum(grad_pre),
        column_sum(upstream_low),
        grad_first_gain,
        grad_first_shift,
        grad_second_gain,
        grad_second_shift,
    ]
    packed = jnp.concatenate(
        [item.astype(jnp.bfloat16).astype(jnp.float32).reshape(count, -1) for item in small],
        axis=1,
    )
    owned = reduce_small(packed)
    pieces = []
    start = 0
    for item in small:
        size = item.shape[0] // count
        pieces.append(owned[start : start + size])
        start += size
    return (
        outputs,
        grad_inputs,
        pair_two[0],
        pair_two[1],
        pair_one[1],
        pair_one[0],
        up_total,
        down_total,
        *pieces,
    )


def solution(mesh):
    return jax.shard_map(
        shards,
        mesh=mesh,
        in_specs=(
            P(("shard", "rep"), None),
            P(("shard", "rep"), None),
            P("shard", None),
            P("shard", None),
            P("shard", None),
            P("shard", None),
            P("shard", None),
            P("shard", None),
            P("shard"),
            P("shard"),
            P("shard"),
            P("shard"),
            P("shard"),
            P("shard"),
            P("shard"),
            P("shard"),
            P("shard"),
            P(("shard", "rep"), None),
        ),
        out_specs=(
            P(("shard", "rep"), None),
            P(("shard", "rep"), None),
            P("shard", None),
            P("shard", None),
            P("shard", None),
            P("shard", None),
            P("shard", None),
            P("shard", None),
            P("shard"),
            P("shard"),
            P("shard"),
            P("shard"),
            P("shard"),
            P("shard"),
            P("shard"),
            P("shard"),
            P("shard"),
        ),
        check_vma=False,
    )
```

```python
from functools import partial

import jax
import jax.numpy as jnp
from jax import lax
from jax.experimental.layout import Layout, with_layout_constraint
from jax.sharding import PartitionSpec as P

H = 17
HD = 64


epsilon = 1e-05


def normalize(values, gain, shift):
    center = values - jnp.mean(values, axis=-1, keepdims=True)
    spread = jnp.mean(center * center, axis=-1, keepdims=True)
    return center * lax.rsqrt(spread + epsilon) * gain + shift


def arrange(lengths, count):
    ends = jnp.cumsum(lengths)
    rowids = jnp.arange(count, dtype=jnp.int32)
    segment = jnp.sum((rowids[:, None] >= ends[None, :]).astype(jnp.int32), axis=1)
    inside = rowids < ends[-1]
    segment = jnp.where(inside, segment, lengths.shape[0] + rowids)
    return (segment, inside.astype(jnp.float32))


def outer(left, right):
    return lax.dot_general(
        left, right, (((0,), (0,)), ((), ())), preferred_element_type=jnp.float32
    )


def inner(left, right):
    return lax.dot_general(
        left, right, (((1,), (1,)), ((), ())), preferred_element_type=jnp.float32
    )


def block_scores(query_block, key_heads, query_segment, segment, start, width):
    key_rows = jnp.arange(segment.shape[0], dtype=jnp.int32)
    query_rows = start + jnp.arange(width, dtype=jnp.int32)
    allowed = (query_segment[:, None] == segment[None, :]) & (
        query_rows[:, None] >= key_rows[None, :]
    )
    scores = (
        jnp.einsum("qhd,khd->hqk", query_block, key_heads, preferred_element_type=jnp.float32)
        * 0.125
    )
    return jnp.where(allowed[None], scores, -1e30)


def attend_forward(queries, keys, values, segment):
    count = queries.shape[0]
    width = min(512, count)
    query_heads = queries.reshape(count, H, HD)
    key_heads = keys.reshape(count, H, HD)
    value_heads = values.reshape(count, H, HD)

    def block(index):
        start = index * width
        scores = block_scores(query_heads, key_heads, segment, segment, start, width)
        highest = jnp.max(scores, axis=-1, keepdims=True)
        expo = jnp.exp(scores - highest)
        total = jnp.sum(expo, axis=-1, keepdims=True)
        weights = (expo / total).astype(jnp.bfloat16)
        result = jnp.einsum(
            "hqk,khd->qhd", weights, value_heads, preferred_element_type=jnp.float32
        )
        return (result, (highest + jnp.log(total))[..., 0])

    results, logsums = lax.map(block, jnp.arange(count // width, dtype=jnp.int32))
    return (results.reshape(count, H * HD), logsums)


def column_sum(values):
    return jnp.sum(values.astype(jnp.float32), axis=0)


def swap(value, axis, bit):
    size = lax.axis_size(axis)
    return lax.ppermute(value, axis, [(i, i ^ bit) for i in range(size)])


def has_bit(axis, bit):
    return (lax.axis_index(axis) // bit) % 2


def tie(*values):
    return lax.optimization_barrier(values)


def halve(value, axis, bit, dim):
    mine = has_bit(axis, bit)
    half = value.shape[dim] // 2
    keep = lax.dynamic_slice_in_dim(value, mine * half, half, dim)
    give = lax.dynamic_slice_in_dim(value, (1 - mine) * half, half, dim)
    got = swap(give, axis, bit)
    return (keep.astype(jnp.float32) + got.astype(jnp.float32)).astype(value.dtype)


def double(value, axis, bit, dim):
    got = swap(value, axis, bit)
    mine = has_bit(axis, bit)
    first = jnp.where(mine == 0, value, got)
    second = jnp.where(mine == 0, got, value)
    return jnp.concatenate([first, second], axis=dim)


def exchange_sum(value, axis, bit):
    return (value.astype(jnp.float32) + swap(value, axis, bit).astype(jnp.float32)).astype(
        value.dtype
    )


def core_stage(term):
    return halve(term, "shard", 1, 1)


def y_stage(term):
    return halve(term, "shard", 2, 0)


def x_stage(term, dim):
    return halve(term, "rep", 1, dim)


def z_stage(term, dim):
    return halve(term, "rep", 2, dim)


def far_stage(term):
    bit = 4
    while bit < lax.axis_size("rep"):
        term = exchange_sum(term, "rep", bit)
        bit *= 2
    return term


def z_back(term, dim):
    return double(term, "rep", 2, dim)


def x_back(term, dim):
    return double(term, "rep", 1, dim)


def finish(term):
    return term.reshape(term.shape[2:]).astype(jnp.float32)


def small_stage(term, axis, bits):
    for bit in bits:
        if bit < lax.axis_size(axis):
            term = exchange_sum(term, axis, bit)
    return term


def place(blocks):
    me = lax.axis_index("shard")
    rows = blocks[0].shape[0]
    full = jnp.zeros((rows * len(blocks),) + blocks[0].shape[1:], blocks[0].dtype)
    for offset, block in enumerate(blocks):
        full = lax.dynamic_update_slice_in_dim(full, block, (me ^ offset) * rows, 0)
    return full


def fetch_half(own):
    half = own.shape[0] // 2
    give = lax.dynamic_slice_in_dim(own, has_bit("rep", 1) * half, half, 0)
    return swap(give, "shard", 2)


def spread(own, got):
    sibling = swap(own, "shard", 1)
    remote = double(got, "rep", 1, 0)
    remote_sibling = swap(remote, "shard", 1)
    return place([own, sibling, remote, remote_sibling])


def shards(
    inputs,
    lengths,
    query_weight,
    key_weight,
    value_weight,
    out_weight,
    up_weight,
    down_weight,
    query_bias,
    value_bias,
    out_bias,
    up_bias,
    down_bias,
    gain_one,
    bias_one,
    gain_two,
    bias_two,
    cotangent,
):
    segment, inside = arrange(lengths[0], inputs.shape[0])
    count = lax.axis_size("shard")
    vectors = [
        query_bias,
        value_bias,
        out_bias,
        gain_one,
        bias_one,
        up_bias,
        down_bias,
        gain_two,
        bias_two,
    ]
    pack = jnp.concatenate(vectors)[None]
    pack_far = swap(pack, "shard", 2)
    pack_near = swap(jnp.concatenate([pack, pack_far]), "shard", 1)
    pack_all = place([pack, pack_near[:1], pack_far, pack_near[1:]]).astype(jnp.float32)
    shifts = []
    start = 0
    for item in vectors:
        shifts.append(pack_all[:, start : start + item.shape[0]].reshape(-1))
        start += item.shape[0]
    query_shift, value_shift, out_shift, first_gain, first_shift = shifts[:5]
    up_shift, down_shift, second_gain, second_shift = shifts[5:]
    got_query, got_key, got_value = (fetch_half(w) for w in (query_weight, key_weight, value_weight))
    full_query = spread(query_weight, got_query)
    full_key = spread(key_weight, got_key)
    full_value = spread(value_weight, got_value)
    got_query, got_key, got_value, out_later, up_later = tie(
        got_query, got_key, got_value, out_weight, up_weight
    )
    got_out, got_up = fetch_half(out_later), fetch_half(up_later)
    full_out = spread(out_later, got_out)
    full_up = spread(up_later, got_up)
    got_up, down_later = tie(got_up, down_weight)
    full_down = spread(down_later, fetch_half(down_later))
    residual = inputs.astype(jnp.float32)
    normed_one = normalize(residual, first_gain, first_shift).astype(jnp.bfloat16)
    queries = (
        jnp.dot(normed_one, full_query, preferred_element_type=jnp.float32) + query_shift
    ).astype(jnp.bfloat16)
    keys = jnp.dot(normed_one, full_key, preferred_element_type=jnp.float32).astype(jnp.bfloat16)
    values = (
        jnp.dot(normed_one, full_value, preferred_element_type=jnp.float32) + value_shift
    ).astype(jnp.bfloat16)
    mixed_float, logsums = attend_forward(queries, keys, values, segment)
    mixed = mixed_float.astype(jnp.bfloat16)
    middle = residual + jnp.dot(mixed, full_out, preferred_element_type=jnp.float32) + out_shift
    normed_two = normalize(middle, second_gain, second_shift).astype(jnp.bfloat16)
    pre_hidden = jnp.dot(normed_two, full_up, preferred_element_type=jnp.float32) + up_shift
    hidden = jax.nn.gelu(pre_hidden, approximate=False).astype(jnp.bfloat16)
    upstream = cotangent.astype(jnp.float32) * inside[:, None]
    upstream_low = upstream.astype(jnp.bfloat16)

    def split(term):
        low = with_layout_constraint(term.astype(jnp.bfloat16), Layout(major_to_minor=(0, 1)))
        return low.reshape(2, 2, -1, term.shape[1])

    def paired(one, two):
        return jnp.stack([split(one), split(two)], axis=2)

    down_sum = core_stage(split(outer(hidden, upstream_low)))
    result = middle + jnp.dot(hidden, full_down, preferred_element_type=jnp.float32) + down_shift
    outputs = (result * inside[:, None]).astype(jnp.bfloat16)
    grad_hidden = inner(upstream_low, full_down)
    _, gelu_pull = jax.vjp(partial(jax.nn.gelu, approximate=False), pre_hidden)
    grad_pre = gelu_pull(grad_hidden)[0].astype(jnp.bfloat16)
    down_sum, grad_pre, outputs = tie(down_sum, grad_pre, outputs)
    down_sum = y_stage(down_sum)
    up_sum = core_stage(split(outer(normed_two, grad_pre)))
    grad_normed_two = inner(grad_pre, full_up)
    _, second_pull = jax.vjp(normalize, middle, second_gain, second_shift)
    grad_middle_norm, grad_second_gain, grad_second_shift = second_pull(grad_normed_two)
    grad_middle = upstream + grad_middle_norm
    grad_branch = grad_middle.astype(jnp.bfloat16)
    grad_mixed = inner(grad_branch, full_out).astype(jnp.bfloat16)
    down_sum, up_sum, grad_mixed, grad_branch = tie(down_sum, up_sum, grad_mixed, grad_branch)
    up_sum = y_stage(up_sum)
    down_sum = x_stage(down_sum, 2)
    grad_out_term = outer(mixed, grad_branch)
    width = queries.shape[0]
    query_heads = queries.reshape(width, H, HD)
    key_heads = keys.reshape(width, H, HD)
    value_heads = values.reshape(width, H, HD)
    grad_heads = grad_mixed.reshape(width, H, HD)
    scores = block_scores(query_heads, key_heads, segment, segment, 0, width)
    probs = jnp.exp(scores - logsums[0][:, :, None])
    grad_values = jnp.einsum(
        "hqk,qhd->khd",
        probs.astype(jnp.bfloat16),
        grad_heads,
        preferred_element_type=jnp.float32,
    ).reshape(width, H * HD).astype(jnp.bfloat16)
    pair_one = paired(grad_out_term, outer(normed_one, grad_values))
    down_sum, up_sum, pair_one, grad_heads = tie(down_sum, up_sum, pair_one, grad_heads)
    pair_one = core_stage(pair_one)
    up_sum = x_stage(up_sum, 2)
    down_sum = z_stage(down_sum, 2)
    grad_probs = jnp.einsum(
        "qhd,khd->hqk", grad_heads, value_heads, preferred_element_type=jnp.float32
    )
    grad_scores = probs * (grad_probs - jnp.sum(probs * grad_probs, axis=-1, keepdims=True))
    grad_scores = (grad_scores * 0.125).astype(jnp.bfloat16)
    down_sum, up_sum, pair_one, grad_scores = tie(down_sum, up_sum, pair_one, grad_scores)
    pair_one = y_stage(pair_one)
    up_sum = z_stage(up_sum, 3)
    down_sum = far_stage(down_sum)
    grad_queries = jnp.einsum(
        "hqk,khd->qhd", grad_scores, key_heads, preferred_element_type=jnp.float32
    ).reshape(width, H * HD).astype(jnp.bfloat16)
    grad_keys = jnp.einsum(
        "hqk,qhd->khd", grad_scores, query_heads, preferred_element_type=jnp.float32
    ).reshape(width, H * HD).astype(jnp.bfloat16)
    pair_two = paired(outer(normed_one, grad_queries), outer(normed_one, grad_keys))
    pair_two, pair_one, up_sum, down_sum, grad_queries, grad_keys = tie(
        pair_two, pair_one, up_sum, down_sum, grad_queries, grad_keys
    )
    pair_two = core_stage(pair_two)
    pair_one = x_stage(pair_one, 3)
    up_sum = far_stage(up_sum)
    down_sum = z_back(down_sum, 2)
    pair_two, pair_one, up_sum, down_sum, grad_queries, grad_keys = tie(
        pair_two, pair_one, up_sum, down_sum, grad_queries, grad_keys
    )
    grad_normed_one = (
        inner(grad_queries, full_query)
        + inner(grad_keys, full_key)
        + inner(grad_values, full_value)
    )
    _, first_pull = jax.vjp(normalize, residual, first_gain, first_shift)
    grad_residual_norm, grad_first_gain, grad_first_shift = first_pull(grad_normed_one)
    grad_inputs = (grad_middle + grad_residual_norm).astype(jnp.bfloat16)
    small = [
        column_sum(grad_queries),
        column_sum(grad_values),
        column_sum(grad_branch),
        column_sum(grad_pre),
        column_sum(upstream_low),
        grad_first_gain,
        grad_first_shift,
        grad_second_gain,
        grad_second_shift,
    ]
    packed = jnp.concatenate(
        [item.astype(jnp.bfloat16).astype(jnp.float32).reshape(count, -1) for item in small],
        axis=1,
    )
    pair_two = y_stage(pair_two)
    pair_one = z_stage(pair_one, 2)
    up_sum = z_back(up_sum, 3)
    down_total = finish(x_back(down_sum, 2))
    pair_two, pair_one, up_sum, packed, grad_inputs = tie(
        pair_two, pair_one, up_sum, packed, grad_inputs
    )
    pair_two = x_stage(pair_two, 3)
    pair_one = far_stage(pair_one)
    up_total = finish(x_back(up_sum, 2))
    packed = small_stage(packed, "shard", (1,))
    pair_two, pair_one, packed = tie(pair_two, pair_one, packed)
    pair_two = z_stage(pair_two, 2)
    pair_one = z_back(pair_one, 2)
    packed = small_stage(packed, "shard", (2,))
    pair_two, pair_one, packed = tie(pair_two, pair_one, packed)
    pair_two = far_stage(pair_two)
    pair_one = finish(x_back(pair_one, 3))
    packed = small_stage(packed, "rep", (1,))
    pair_two, packed = tie(pair_two, packed)
    pair_two = z_back(pair_two, 2)
    packed = small_stage(packed, "rep", (2,))
    pair_two, packed = tie(pair_two, packed)
    pair_two = finish(x_back(pair_two, 3))
    packed = small_stage(packed, "rep", (4, 8, 16, 32, 64, 128))
    owned = lax.dynamic_index_in_dim(packed, lax.axis_index("shard"), 0, keepdims=False)
    pieces = []
    start = 0
    for item in small:
        size = item.shape[0] // count
        pieces.append(owned[start : start + size])
        start += size
    return (
        outputs,
        grad_inputs,
        pair_two[0],
        pair_two[1],
        pair_one[1],
        pair_one[0],
        up_total,
        down_total,
        *pieces,
    )


def solution(mesh):
    return jax.shard_map(
        shards,
        mesh=mesh,
        in_specs=(
            P(("shard", "rep"), None),
            P(("shard", "rep"), None),
            P("shard", None),
            P("shard", None),
            P("shard", None),
            P("shard", None),
            P("shard", None),
            P("shard", None),
            P("shard"),
            P("shard"),
            P("shard"),
            P("shard"),
            P("shard"),
            P("shard"),
            P("shard"),
            P("shard"),
            P("shard"),
            P(("shard", "rep"), None),
        ),
        out_specs=(
            P(("shard", "rep"), None),
            P(("shard", "rep"), None),
            P("shard", None),
            P("shard", None),
            P("shard", None),
            P("shard", None),
            P("shard", None),
            P("shard", None),
            P("shard"),
            P("shard"),
            P("shard"),
            P("shard"),
            P("shard"),
            P("shard"),
            P("shard"),
            P("shard"),
            P("shard"),
        ),
        check_vma=False,
    )
```
